32 devices in a mesh: section: 2 (over x), tensor: 4 (over y, core), dp: 4 (over z).
Axes of the slice: x: 2, y: 2, z: 4, core: 2. Of those that a mesh axis runs over, the one named last changes fastest.
Arguments:
- tokens: bfloat16 [4, 8, 257, 1024], P(None, 'dp'), may hold values from -6 to 6
- cotangent: bfloat16 [4, 8, 257, 1024], P(None, 'dp'), may hold values from -6 to 6
- vectors: bfloat16 [2, 8, 1024], P('section'), may hold values from -0.5 to 1.5, as said below
- w_qkv: bfloat16 [2, 3, 1024, 1024], P('section', None, None, 'tensor'), may hold values from -0.1875 to 0.1875
- qv_bias: bfloat16 [2, 2, 1024], P('section', None, 'tensor'), may hold values from -2 to 2
- w_out: bfloat16 [2, 1024, 1024], P('section', 'tensor'), may hold values from -0.75 to 0.75
- w_fc1: bfloat16 [2, 1024, 4096], P('section', None, 'tensor'), may hold values from -0.1875 to 0.1875
- fc1_bias: bfloat16 [2, 4096], P('section', 'tensor'), may hold values from -2 to 2
- w_fc2: bfloat16 [2, 4096, 1024], P('section', 'tensor'), may hold values from -0.09375 to 0.09375
Outputs:
- section_outputs: bfloat16 [2, 4, 8, 257, 1024], P('section', None, 'dp')
- input_grads: float32 [2, 4, 8, 257, 1024], P('section', None, 'dp')
- grad_vectors: float32 [2, 8, 1024], P('section')
- grad_qkv: float32 [2, 3, 1024, 1024], P('section', None, None, 'tensor')
- grad_qv_bias: float32 [2, 2, 1024], P('section', None, 'tensor')
- grad_out: float32 [2, 1024, 1024], P('section', 'tensor')
- grad_fc1: float32 [2, 1024, 4096], P('section', None, 'tensor')
- grad_fc1_bias: float32 [2, 4096], P('section', 'tensor')
- grad_fc2: float32 [2, 4096, 1024], P('section', 'tensor')
The draws below stay inside these ranges and needn't reach their ends.
Inputs may be any that keep to these rules, and one draw needn't show every extreme that they name: `vectors`: rows 0, 3, 4 and 7 of each layer lie around one, the other rows around zero.
All inputs are finite; a program needn't handle non-finite values.
Results may differ from the reference program's by a relative error of at most 0.03.
Values may be sent and summed in bfloat16 or wider, within the bound.
A program may use at most 256 MiB of HBM per device.

```python
import jax
import jax.numpy as jnp
from jax import lax

D = 1024
HD = 64
FF = 4096
SEQ = 257
MICRO = 4
IMAGES = 8
N_TENSOR = 4


def draw_vectors(key, part):
    key = jax.random.fold_in(key, 11)
    base = jnp.clip(jax.random.normal(key, (2, 8, D), jnp.float32), -2.5, 2.5) * 0.5
    is_gain = jnp.array([1.0, 0.0, 0.0, 1.0, 1.0, 0.0, 0.0, 1.0], jnp.float32)[None, :, None]
    return (is_gain * (1.0 + 0.4 * base) + (1.0 - is_gain) * (0.4 * base)).astype(jnp.bfloat16)


def block_scale(rng, extent, shards, smallest, high):
    loudness, own = 1.0, jax.random.fold_in(rng, 6)
    for dim, shards_of in shards:
        steps = jnp.exp(jax.random.uniform(jax.random.fold_in(own, dim), (shards_of,), jnp.float32, smallest / len(shards), high / len(shards)))
        loudness = loudness * jnp.repeat(steps, extent[dim] // shards_of).reshape([-1 if axis == dim else 1 for axis in range(len(extent))])
    return loudness


def scatter_about(own_key, dims, spread, reach, split=(), held_as=jnp.bfloat16):
    level = block_scale(own_key, dims, split, -0.22, 0.18) if split else 1.0
    values = jax.random.normal(own_key, dims, jnp.float32) * spread * level
    return jnp.minimum(jnp.maximum(values, -reach), reach).astype(held_as)


def setup_inputs(seed: int = 0) -> dict:
    seeds = jax.random.split(jax.random.key(seed), 10)
    tokens = scatter_about(seeds[0], (MICRO, IMAGES, SEQ, D), 1.0, 6.0, ((1, 4),))
    cotangent = scatter_about(seeds[1], (MICRO, IMAGES, SEQ, D), 1.0, 6.0, ((1, 4),))
    vectors = draw_vectors(jax.random.fold_in(seeds[9], 71), 0)
    w_qkv = scatter_about(seeds[3], (2, 3, D, D), D ** -0.5, 0.1875, ((0, 2), (3, 4)))
    qv_bias = scatter_about(seeds[4], (2, 2, D), 0.3, 2.0, ((0, 2), (2, 4)))
    w_out = scatter_about(seeds[5], (2, D, D), (D // 16) ** -0.5, 0.75, ((0, 2), (1, 4)))
    w_fc1 = scatter_about(seeds[6], (2, D, FF), D ** -0.5, 0.1875, ((0, 2), (2, 4)))
    fc1_bias = scatter_about(seeds[7], (2, FF), 0.3, 2.0, ((0, 2), (1, 4)))
    w_fc2 = scatter_about(seeds[8], (2, FF, D), FF ** -0.5, 0.09375, ((0, 2), (1, 4)))
    return dict(tokens=tokens, cotangent=cotangent, vectors=vectors, w_qkv=w_qkv, qv_bias=qv_bias, w_out=w_out, w_fc1=w_fc1, fc1_bias=fc1_bias, w_fc2=w_fc2)


@jax.custom_vjp
def low(v):
    return lax.optimization_barrier(v.astype(jnp.bfloat16)).astype(jnp.float32)

@jax.custom_vjp
def low_back(v):
    return v

def low_keep(v):
    return (low(v), None)

def low_pass(kept, grad):
    return (grad,)

def back_keep(v):
    return (v, None)

def back_low(kept, grad):
    return (low(grad),)
low.defvjp(low_keep, low_pass)
low_back.defvjp(back_keep, back_low)
eps_norm = 1e-06

def high_dot(left, right):
    return jnp.dot(left, right, precision=lax.Precision.HIGHEST, preferred_element_type=jnp.float32)

def normalize(values, gain, shift):
    center = values - lax.optimization_barrier(jnp.mean(values, axis=-1, keepdims=True))
    inverse = lax.rsqrt(lax.optimization_barrier(jnp.mean(center * center, axis=-1, keepdims=True)) + eps_norm)
    return center * inverse * gain + shift

def attend_image(triple):
    queries, key_rows, value_rows = triple
    scores = low_back(jnp.einsum('qhd,khd->hqk', queries, key_rows, precision=lax.Precision.HIGHEST) * HD ** (-0.5))
    highest = lax.optimization_barrier(jnp.max(scores, axis=-1, keepdims=True))
    raised = jnp.exp(scores - highest)
    probs = raised / lax.optimization_barrier(jnp.sum(raised, axis=-1, keepdims=True))
    return jnp.einsum('hqk,khd->qhd', low(probs), value_rows, precision=lax.Precision.HIGHEST)

def layer(vector_rows, qkv_weight, bias_pair, out_weight, fc1_weight, fc1_shift, fc2_weight, stream):
    images, seq_len, model_width = stream.shape
    token_rows = stream.reshape(images * seq_len, model_width)
    normed = low(normalize(token_rows, vector_rows[0], vector_rows[1]))
    col_share = model_width // N_TENSOR
    head_shape = (images, seq_len, col_share // HD, HD)
    attended = jnp.zeros_like(token_rows)
    for group_no in range(N_TENSOR):
        lower_col = group_no * col_share
        upper_col = lower_col + col_share
        group_input = low_back(normed)
        queries = low(low_back(high_dot(group_input, qkv_weight[0][:, lower_col:upper_col]) + bias_pair[0][lower_col:upper_col]))
        key_rows = low(low_back(high_dot(group_input, qkv_weight[1][:, lower_col:upper_col])))
        value_rows = low(low_back(high_dot(group_input, qkv_weight[2][:, lower_col:upper_col]) + bias_pair[1][lower_col:upper_col]))
        mixed = lax.map(jax.checkpoint(attend_image), (queries.reshape(head_shape), key_rows.reshape(head_shape), value_rows.reshape(head_shape)))
        mixed = low(low_back(mixed.reshape(images * seq_len, col_share)))
        attended = attended + low(high_dot(mixed, out_weight[lower_col:upper_col, :]))
    attended = low_back(attended)
    after_attn = token_rows + vector_rows[3] * (attended + vector_rows[2])
    normed_two = low(normalize(after_attn, vector_rows[4], vector_rows[5]))
    unit_share = FF // N_TENSOR
    mlp_out = jnp.zeros_like(token_rows)
    for group_no in range(N_TENSOR):
        lower_col = group_no * unit_share
        upper_col = lower_col + unit_share
        group_input = low_back(normed_two)
        hidden_pre = low_back(high_dot(group_input, fc1_weight[:, lower_col:upper_col]) + fc1_shift[lower_col:upper_col])
        hidden_low = low(jax.nn.gelu(hidden_pre, approximate=False))
        mlp_out = mlp_out + low(high_dot(hidden_low, fc2_weight[lower_col:upper_col, :]))
    mlp_out = low_back(mlp_out)
    result = after_attn + vector_rows[7] * (mlp_out + vector_rows[6])
    return result.reshape(images, seq_len, model_width)

def reference(tokens, cotangent, vectors, w_qkv, qv_bias, w_out, w_fc1, fc1_bias, w_fc2):
    micro_count, images, seq_len, model_width = tokens.shape
    params = tuple((weight.astype(jnp.float32) for weight in (vectors, w_qkv, qv_bias, w_out, w_fc1, fc1_bias, w_fc2)))
    start_in = tokens.astype(jnp.float32).reshape(micro_count * images, seq_len, model_width)
    opening = jnp.zeros_like(start_in)

    def forward(params, start_in, opening):
        first_out = layer(*[weight[0] for weight in params], start_in)
        middle = low_back(low(first_out)) + opening
        last_out = layer(*[weight[1] for weight in params], middle)
        return (last_out, first_out)
    last_out, pullback, first_out = jax.vjp(forward, params, start_in, opening, has_aux=True)
    grad_params, grad_start, grad_middle = pullback(cotangent.astype(jnp.float32).reshape(last_out.shape))
    shape_out = (2, micro_count, images, seq_len, model_width)
    section_outputs = jnp.stack([first_out, last_out]).reshape(shape_out).astype(jnp.bfloat16)
    input_grads = jnp.stack([grad_start, grad_middle]).reshape(shape_out)
    return (section_outputs, input_grads, grad_params[0], grad_params[1], grad_params[2], grad_params[3], grad_params[4], grad_params[5], grad_params[6])
```

```python
from functools import partial

import jax
import jax.numpy as jnp
from jax import lax
from jax.experimental import pallas as pl
from jax.experimental.pallas import tpu as pltpu
from jax.sharding import PartitionSpec as P

HD = 64
LAG = 2
EPS = 1e-06
LOW = jnp.bfloat16
F32 = jnp.float32
VMEM_BYTES = 40 * 1024 * 1024


def dot_nn(a, b):
    return jnp.dot(a, b, preferred_element_type=F32)


def dot_tn(a, b):
    return lax.dot_general(a, b, (((0,), (0,)), ((), ())), preferred_element_type=F32)


def dot_nt(a, b):
    return lax.dot_general(a, b, (((1,), (1,)), ((), ())), preferred_element_type=F32)


def unit_rows_of(x):
    center = x - jnp.mean(x, axis=-1, keepdims=True)
    inverse = lax.rsqrt(jnp.mean(center * center, axis=-1, keepdims=True) + EPS)
    return center * inverse, inverse


def norm_back(upstream, unit, inverse, gain):
    scaled = upstream * gain
    inner = jnp.mean(scaled * unit, axis=-1, keepdims=True)
    return inverse * (scaled - jnp.mean(scaled, axis=-1, keepdims=True) - unit * inner)


def col_sum(x):
    return jnp.sum(x, axis=0, keepdims=True)


def split_out(flags, part, mine_ref, send_ref):
    half = part.shape[1] // 2
    low_core = flags[1] == 0
    lo, hi = part[:, :half], part[:, half:]
    mine_ref[...] = jnp.where(low_core, lo, hi).astype(LOW)
    send_ref[...] = jnp.where(low_core, hi, lo).astype(LOW)


def join(flags, mine_ref, other_ref):
    low_core = flags[1] == 0
    mine, other = mine_ref[...].astype(F32), other_ref[...].astype(F32)
    return jnp.concatenate(
        [jnp.where(low_core, mine, other), jnp.where(low_core, other, mine)], axis=1
    )


def probs_of(q, k, seq):
    s = dot_nt(q, k) * HD ** (-0.5)
    cols = lax.broadcasted_iota(jnp.int32, s.shape, 1)
    s = jnp.where(cols < seq, s, -1e30)
    e = jnp.exp(s - jnp.max(s, axis=-1, keepdims=True))
    return e * (1.0 / jnp.sum(e, axis=-1, keepdims=True))


def attn_fwd_kernel(seq, flags, own, arrived, vec, wqkv, qvb, wout, x_o, n1_o, qkv_o, o_o, mine_o, send_o):
    x16 = jnp.where(flags[0] == 1, own[0].astype(F32), arrived[0].astype(F32))
    x_o[...] = x16.astype(LOW)
    unit, _ = unit_rows_of(x16)
    n1 = (unit * vec[0:1, :] + vec[1:2, :]).astype(LOW)
    n1_o[...] = n1
    share = wqkv.shape[2]
    q = (dot_nn(n1, wqkv[0]) + qvb[0:1, :]).astype(LOW)
    k = dot_nn(n1, wqkv[1]).astype(LOW)
    v = (dot_nn(n1, wqkv[2]) + qvb[1:2, :]).astype(LOW)
    qkv_o[:, 0:share] = q
    qkv_o[:, share : 2 * share] = k
    qkv_o[:, 2 * share :] = v
    heads = []
    for h in range(share // HD):
        cut = slice(h * HD, (h + 1) * HD)
        p = probs_of(q[:, cut], k[:, cut], seq).astype(LOW)
        heads.append(dot_nn(p, v[:, cut]))
    o = jnp.concatenate(heads, axis=1).astype(LOW)
    o_o[...] = o
    split_out(flags, dot_nn(o, wout[...]), mine_o, send_o)


def mlp_fwd_kernel(flags, x, a_m, a_s, vec, fc1, fc1b, fc2, n2_o, g_o, dg_o, mine_o, send_o):
    a = join(flags, a_m, a_s)
    h1 = x[...].astype(F32) + vec[3:4, :] * (a + vec[2:3, :])
    unit, _ = unit_rows_of(h1)
    n2 = (unit * vec[4:5, :] + vec[5:6, :]).astype(LOW)
    n2_o[...] = n2
    width = fc1.shape[1]
    chunk = min(width, 256)
    total = None
    for c in range(0, width, chunk):
        cut = slice(c, c + chunk)
        u = dot_nn(n2, fc1[:, cut]) + fc1b[:, cut]
        phi = 0.5 * (1.0 + lax.erf(u * (2.0 ** -0.5)))
        g = (u * phi).astype(LOW)
        g_o[:, cut] = g
        dens = jnp.exp(-0.5 * u * u) * 0.3989422804014327
        dg_o[:, cut] = (phi + u * dens).astype(LOW)
        term = dot_nn(g, fc2[cut, :])
        total = term if total is None else total + term
    split_out(flags, total, mine_o, send_o)


def out_kernel(flags, x, a_m, a_s, m_m, m_s, vec, y_o):
    h1 = x[...].astype(F32) + vec[3:4, :] * (join(flags, a_m, a_s) + vec[2:3, :])
    y_o[0] = (h1 + vec[7:8, :] * (join(flags, m_m, m_s) + vec[6:7, :])).astype(LOW)


def mlp_bwd_kernel(flags, cot, returned, m_m, m_s, dg, vec, fc1, fc2, dy_o, dm_o, du_o, mine_o, send_o, sums_o):
    dy = jnp.where(flags[0] == 1, returned[0].astype(F32), cot[0].astype(F32))
    dy_o[...] = dy.astype(LOW)
    m = join(flags, m_m, m_s)
    scaled = dy * vec[7:8, :]
    sums_o[0:1, :] = col_sum(scaled)
    sums_o[1:2, :] = col_sum(dy * (m + vec[6:7, :]))
    dm = scaled.astype(LOW)
    dm_o[...] = dm
    width = fc1.shape[1]
    chunk = min(width, 256)
    total = None
    for c in range(0, width, chunk):
        cut = slice(c, c + chunk)
        du = (dot_nt(dm, fc2[cut, :]) * dg[:, cut].astype(F32)).astype(LOW)
        du_o[:, cut] = du
        sums_o[2:3, cut] = col_sum(du.astype(F32))
        term = dot_nt(du, fc1[:, cut])
        total = term if total is None else total + term
    split_out(flags, total, mine_o, send_o)


def attn_bwd_kernel(
    seq, flags, x, a_m, a_s, dy, d_m, d_s, qkv, vec, wqkv, wout, dh_o, da_o, dqkv_o, mine_o, send_o, sums_o, pair_o
):
    a = join(flags, a_m, a_s) + vec[2:3, :]
    h1 = x[...].astype(F32) + vec[3:4, :] * a
    unit, inverse = unit_rows_of(h1)
    dn2 = join(flags, d_m, d_s)
    sums_o[0:1, :] = col_sum(dn2 * unit)
    sums_o[1:2, :] = col_sum(dn2)
    dh1 = dy[...].astype(F32) + norm_back(dn2, unit, inverse, vec[4:5, :])
    dh_o[...] = dh1
    scaled = dh1 * vec[3:4, :]
    sums_o[2:3, :] = col_sum(scaled)
    sums_o[3:4, :] = col_sum(dh1 * a)
    da = scaled.astype(LOW)
    da_o[...] = da
    do = dot_nt(da, wout[...]).astype(LOW)
    share = wqkv.shape[2]
    dqs, dks, dvs = [], [], []
    for h in range(share // HD):
        cut = slice(h * HD, (h + 1) * HD)
        q = qkv[:, h * HD : (h + 1) * HD]
        k = qkv[:, share + h * HD : share + (h + 1) * HD]
        v = qkv[:, 2 * share + h * HD : 2 * share + (h + 1) * HD]
        p = probs_of(q, k, seq)
        dvs.append(dot_tn(p.astype(LOW), do[:, cut]))
        dp = dot_nt(do[:, cut], v)
        ds = (p * (dp - jnp.sum(p * dp, axis=-1, keepdims=True))).astype(LOW)
        dqs.append(dot_nn(ds, k) * HD ** (-0.5))
        dks.append(dot_tn(ds, q) * HD ** (-0.5))
    dq = jnp.concatenate(dqs, axis=1).astype(LOW)
    dk = jnp.concatenate(dks, axis=1).astype(LOW)
    dv = jnp.concatenate(dvs, axis=1).astype(LOW)
    dqkv_o[:, 0:share] = dq
    dqkv_o[:, share : 2 * share] = dk
    dqkv_o[:, 2 * share :] = dv
    pair_o[0:1, :] = col_sum(dq.astype(F32))
    pair_o[1:2, :] = col_sum(dv.astype(F32))
    split_out(flags, dot_nt(dq, wqkv[0]) + dot_nt(dk, wqkv[1]) + dot_nt(dv, wqkv[2]), mine_o, send_o)


def in_bwd_kernel(flags, x, dh, d_m, d_s, vec, dx_o, low_o, sums_o):
    unit, inverse = unit_rows_of(x[...].astype(F32))
    dn1 = join(flags, d_m, d_s)
    sums_o[0:1, :] = col_sum(dn1 * unit)
    sums_o[1:2, :] = col_sum(dn1)
    dx = dh[...] + norm_back(dn1, unit, inverse, vec[0:1, :])
    dx_o[...] = dx[: dx_o.shape[0]]
    low_o[0] = dx.astype(LOW)


def weight_kernel(count, *refs):
    lefts, rights, out = refs[:count], refs[count : 2 * count], refs[2 * count]
    total = dot_tn(lefts[0][...], rights[0][...])
    for n in range(1, count):
        total = total + dot_tn(lefts[n][...], rights[n][...])
    out[0] = total.astype(out.dtype)


def whole(shape, block=None, pick=None):
    block = shape if block is None else block
    at = (0,) * len(shape) if pick is None else pick
    return pl.BlockSpec(block, lambda i: at)


def call(kernel, args, outs, picks=None, flops=0):
    picks = picks or {}
    specs = [pl.BlockSpec(memory_space=pltpu.SMEM)]
    for n, arg in enumerate(args[1:], 1):
        if n in picks:
            specs.append(whole(arg.shape, (1,) + arg.shape[1:], (picks[n], 0, 0)))
        else:
            specs.append(whole(arg.shape))
    moved = sum(a.size * a.dtype.itemsize for a in args[1:])
    return pl.pallas_call(
        kernel,
        grid=(1,),
        in_specs=specs,
        out_specs=[whole(s.shape) for s in outs],
        out_shape=outs,
        compiler_params=pltpu.CompilerParams(vmem_limit_bytes=VMEM_BYTES),
        cost_estimate=pl.CostEstimate(flops=flops, bytes_accessed=moved, transcendentals=0),
    )(*args)


def weight_grad(lefts, rights, blocks):
    count = len(lefts)
    rows, depth = lefts[0].shape
    width = rights[0].shape[1]
    block = width // blocks
    return pl.pallas_call(
        partial(weight_kernel, count),
        grid=(blocks,),
        in_specs=[pl.BlockSpec((rows, depth), lambda i: (0, 0))] * count
        + [pl.BlockSpec((rows, block), lambda i: (0, i))] * count,
        out_specs=pl.BlockSpec((1, depth, block), lambda i: (i, 0, 0)),
        out_shape=jax.ShapeDtypeStruct((blocks, depth, block), LOW),
        compiler_params=pltpu.CompilerParams(vmem_limit_bytes=VMEM_BYTES),
        cost_estimate=pl.CostEstimate(
            flops=2 * count * rows * depth * width,
            bytes_accessed=2 * count * rows * (depth + width) + 2 * depth * width,
            transcendentals=0,
        ),
    )(*lefts, *rights)


def swap(value, bit):
    route = [(i, i ^ bit) for i in range(lax.axis_size("tensor"))]
    return lax.ppermute(value, "tensor", route)


def tensor_sum(mine, send):
    size = lax.axis_size("tensor")
    got = swap(send, 1)
    held = (mine.astype(F32) + got.astype(F32)).astype(LOW)
    bit = 2
    while bit < size:
        got = swap(held, bit)
        held = (held.astype(F32) + got.astype(F32)).astype(LOW)
        bit *= 2
    return held, swap(held, 1)


def passed_along(block, distance):
    devices = range(lax.axis_size("section"))
    route = [(i - distance, i) for i in devices if i - distance in devices]
    return lax.ppermute(block, "section", route)


def body(tokens, cotangent, vectors, w_qkv, qv_bias, w_out, w_fc1, fc1_bias, w_fc2):
    micro_count, images, seq, width = tokens.shape
    units = micro_count * images
    rows = -(-seq // 16) * 16
    wqkv, wout, fc1, fc2 = w_qkv[0], w_out[0], w_fc1[0], w_fc2[0]
    share, hidden = wqkv.shape[2], fc1.shape[1]
    vec = vectors[0].astype(F32)
    qvb = qv_bias[0].astype(F32)
    fc1b = fc1_bias.astype(F32)
    first = lax.axis_index("section") == 0
    flags = jnp.stack([first.astype(jnp.int32), (lax.axis_index("tensor") % 2).astype(jnp.int32)])
    pad = ((0, 0), (0, rows - seq), (0, 0))
    own = jnp.pad(tokens.reshape(units, seq, width), pad)
    cot = jnp.pad(cotangent.reshape(units, seq, width), pad)
    zeros = jnp.zeros((1, rows, width), LOW)

    def low(*shape):
        return jax.ShapeDtypeStruct(shape, LOW)

    def wide(*shape):
        return jax.ShapeDtypeStruct(shape, F32)

    halves = [low(rows, width // 2)] * 2
    ticks = units + LAG
    unit_flops = 2 * rows * width
    arrivals, results, records = {}, [], []
    for t in range(ticks):
        x, n1, qkv, o, mine, send = call(
            partial(attn_fwd_kernel, seq),
            (flags, own if t < units else zeros, arrivals.get(t, zeros), vec, wqkv, qvb, wout),
            [low(rows, width), low(rows, width), low(rows, 3 * share), low(rows, share)] + halves,
            {1: t} if t < units else None,
            unit_flops * share * 8,
        )
        a_m, a_s = tensor_sum(mine, send)
        n2, g, dg, mine, send = call(
            mlp_fwd_kernel,
            (flags, x, a_m, a_s, vec, fc1, fc1b, fc2),
            [low(rows, width), low(rows, hidden), low(rows, hidden)] + halves,
            flops=unit_flops * hidden * 3,
        )
        m_m, m_s = tensor_sum(mine, send)
        (y,) = call(out_kernel, (flags, x, a_m, a_s, m_m, m_s, vec), [low(1, rows, width)])
        results.append(y)
        if t + LAG < ticks:
            arrivals[t + LAG] = passed_along(y, 1)
        records.append((x, n1, qkv, o, a_m, a_s, n2, g, dg, m_m, m_s))

    returns, grads, small = {}, [], []
    pieces = [[] for _ in range(4)]
    for t in range(ticks):
        x, n1, qkv, o, a_m, a_s, n2, g, dg, m_m, m_s = records[ticks - 1 - t]
        dy, dm, du, mine, send, sums_mlp = call(
            mlp_bwd_kernel,
            (flags, cot if t < units else zeros, returns.get(t, zeros), m_m, m_s, dg, vec, fc1, fc2),
            [low(rows, width), low(rows, width), low(rows, hidden)] + halves + [wide(3, width)],
            {1: units - 1 - t} if t < units else None,
            unit_flops * hidden * 2,
        )
        d_m, d_s = tensor_sum(mine, send)
        dh, da, dqkv, mine, send, sums_attn, pair = call(
            partial(attn_bwd_kernel, seq),
            (flags, x, a_m, a_s, dy, d_m, d_s, qkv, vec, wqkv, wout),
            [wide(rows, width), low(rows, width), low(rows, 3 * share)] + halves + [wide(4, width), wide(2, share)],
            flops=unit_flops * share * 10,
        )
        d_m, d_s = tensor_sum(mine, send)
        dx, dx_low, sums_in = call(
            in_bwd_kernel,
            (flags, x, dh, d_m, d_s, vec),
            [wide(seq, width), low(1, rows, width), wide(2, width)],
        )
        grads.append(dx)
        if t + LAG < ticks:
            returns[t + LAG] = passed_along(dx_low, -1)
        small.append((sums_mlp, sums_attn, sums_in, pair))
        for piece, pairing in zip(pieces, ((g, dm), (n2, du), (o, da), (n1, dqkv))):
            piece.append(pairing)

    blocks = (2, 2, 2, 3)
    grad_fc2, grad_fc1, grad_out, grad_qkv = [
        weight_grad([p[0] for p in piece], [p[1] for p in piece], n)
        for piece, n in zip(pieces, blocks)
    ]
    sums_mlp, sums_attn, sums_in, pair = [sum(s[1:], s[0]) for s in zip(*small)]
    grad_vec = jnp.concatenate([sums_in, sums_attn[2:4], sums_attn[0:2], sums_mlp[0:2]], axis=0)
    summed = lax.psum(
        (
            grad_fc2,
            grad_fc1,
            grad_qkv,
            grad_out,
            grad_vec.astype(LOW),
            sums_mlp[2:3].astype(LOW),
            pair.astype(LOW),
        ),
        "dp",
    )
    grad_fc2, grad_fc1, grad_qkv, grad_out, grad_vec, grad_fc1b, grad_pair = [
        s.astype(F32) for s in summed
    ]

    def columns(blocked):
        return jnp.concatenate([blocked[n] for n in range(blocked.shape[0])], axis=1)

    shape_out = (1, micro_count, images, seq, width)
    outputs = jnp.stack(
        [jnp.where(first, results[m][0, :seq], results[m + LAG][0, :seq]) for m in range(units)]
    ).reshape(shape_out)
    input_grads = jnp.stack(
        [jnp.where(first, grads[ticks - 1 - m], grads[units - 1 - m]) for m in range(units)]
    ).reshape(shape_out)
    return (
        outputs,
        input_grads,
        grad_vec[None],
        grad_qkv[None],
        grad_pair[None],
        columns(grad_out)[None],
        columns(grad_fc1)[None],
        grad_fc1b,
        columns(grad_fc2)[None],
    )


def solution(mesh):
    return jax.shard_map(
        body,
        mesh=mesh,
        in_specs=(
            P(None, "dp", None, None),
            P(None, "dp", None, None),
            P("section", None, None),
            P("section", None, None, "tensor"),
            P("section", None, "tensor"),
            P("section", "tensor", None),
            P("section", None, "tensor"),
            P("section", "tensor"),
            P("section", "tensor", None),
        ),
        out_specs=(
            P("section", None, "dp", None, None),
            P("section", None, "dp", None, None),
            P("section", None, None),
            P("section", None, None, "tensor"),
            P("section", None, "tensor"),
            P("section", "tensor", None),
            P("section", None, "tensor"),
            P("section", "tensor"),
            P("section", "tensor", None),
        ),
        check_vma=False,
    )
```

```python
from functools import partial

import jax
import jax.numpy as jnp
from jax import lax
from jax.experimental import pallas as pl
from jax.experimental.pallas import tpu as pltpu
from jax.sharding import PartitionSpec as P

HD = 64
LAG = 2
EPS = 1e-06
LOW = jnp.bfloat16
F32 = jnp.float32
VMEM_BYTES = 40 * 1024 * 1024


def dot_nn(a, b):
    return jnp.dot(a, b, preferred_element_type=F32)


def dot_tn(a, b):
    return lax.dot_general(a, b, (((0,), (0,)), ((), ())), preferred_element_type=F32)


def dot_nt(a, b):
    return lax.dot_general(a, b, (((1,), (1,)), ((), ())), preferred_element_type=F32)


def unit_rows_of(x):
    center = x - jnp.mean(x, axis=-1, keepdims=True)
    inverse = lax.rsqrt(jnp.mean(center * center, axis=-1, keepdims=True) + EPS)
    return center * inverse, inverse


def norm_back(upstream, unit, inverse, gain):
    scaled = upstream * gain
    inner = jnp.mean(scaled * unit, axis=-1, keepdims=True)
    return inverse * (scaled - jnp.mean(scaled, axis=-1, keepdims=True) - unit * inner)


def col_sum(x):
    return jnp.sum(x, axis=0, keepdims=True)


def split_out(flags, part, mine_ref, send_ref):
    half = part.shape[1] // 2
    low_core = flags[1] == 0
    lo, hi = part[:, :half], part[:, half:]
    mine_ref[...] = jnp.where(low_core, lo, hi).astype(LOW)
    send_ref[...] = jnp.where(low_core, hi, lo).astype(LOW)


def own_half(flags, full):
    half = full.shape[1] // 2
    return jnp.where(flags[1] == 0, full[:, :half], full[:, half:]).astype(LOW)


def join(flags, mine_ref, other_ref):
    low_core = flags[1] == 0
    mine, other = mine_ref[...].astype(F32), other_ref[...].astype(F32)
    return jnp.concatenate(
        [jnp.where(low_core, mine, other), jnp.where(low_core, other, mine)], axis=1
    )


def probs_of(q, k, seq):
    s = dot_nt(q, k) * HD ** (-0.5)
    cols = lax.broadcasted_iota(jnp.int32, s.shape, 1)
    s = jnp.where(cols < seq, s, -1e30)
    e = jnp.exp(s - jnp.max(s, axis=-1, keepdims=True))
    return e * (1.0 / jnp.sum(e, axis=-1, keepdims=True))


def attn_fwd_kernel(seq, flags, own, arr_m, arr_s, vec, wqkv, qvb, wout, x_o, n1_o, qkv_o, o_o, mine_o, send_o):
    x16 = jnp.where(flags[0] == 1, own[0].astype(F32), join(flags, arr_m, arr_s))
    x_o[...] = x16.astype(LOW)
    unit, _ = unit_rows_of(x16)
    n1 = (unit * vec[0:1, :] + vec[1:2, :]).astype(LOW)
    n1_o[...] = n1
    share = wqkv.shape[2]
    q = (dot_nn(n1, wqkv[0]) + qvb[0:1, :]).astype(LOW)
    k = dot_nn(n1, wqkv[1]).astype(LOW)
    v = (dot_nn(n1, wqkv[2]) + qvb[1:2, :]).astype(LOW)
    qkv_o[:, 0:share] = q
    qkv_o[:, share : 2 * share] = k
    qkv_o[:, 2 * share :] = v
    heads = []
    for h in range(share // HD):
        cut = slice(h * HD, (h + 1) * HD)
        p = probs_of(q[:, cut], k[:, cut], seq).astype(LOW)
        heads.append(dot_nn(p, v[:, cut]))
    o = jnp.concatenate(heads, axis=1).astype(LOW)
    o_o[...] = o
    split_out(flags, dot_nn(o, wout[...]), mine_o, send_o)


def mlp_fwd_kernel(flags, x, a_m, a_s, vec, fc1, fc1b, fc2, n2_o, g_o, dg_o, mine_o, send_o):
    a = join(flags, a_m, a_s)
    h1 = x[...].astype(F32) + vec[3:4, :] * (a + vec[2:3, :])
    unit, _ = unit_rows_of(h1)
    n2 = (unit * vec[4:5, :] + vec[5:6, :]).astype(LOW)
    n2_o[...] = n2
    width = fc1.shape[1]
    chunk = min(width, 256)
    total = None
    for c in range(0, width, chunk):
        cut = slice(c, c + chunk)
        u = dot_nn(n2, fc1[:, cut]) + fc1b[:, cut]
        phi = 0.5 * (1.0 + lax.erf(u * (2.0 ** -0.5)))
        g = (u * phi).astype(LOW)
        g_o[:, cut] = g
        dens = jnp.exp(-0.5 * u * u) * 0.3989422804014327
        dg_o[:, cut] = (phi + u * dens).astype(LOW)
        term = dot_nn(g, fc2[cut, :])
        total = term if total is None else total + term
    split_out(flags, total, mine_o, send_o)


def out_kernel(flags, x, a_m, a_s, m_m, m_s, vec, y_o, half_o):
    h1 = x[...].astype(F32) + vec[3:4, :] * (join(flags, a_m, a_s) + vec[2:3, :])
    y = h1 + vec[7:8, :] * (join(flags, m_m, m_s) + vec[6:7, :])
    y_o[...] = y.astype(LOW)
    half_o[...] = own_half(flags, y)


def mlp_bwd_kernel(flags, cot, ret_m, ret_s, m_m, m_s, dg, vec, fc1, fc2, dy_o, dm_o, du_o, mine_o, send_o, sums_o):
    dy = jnp.where(flags[0] == 1, join(flags, ret_m, ret_s), cot[0].astype(F32))
    dy_o[...] = dy.astype(LOW)
    m = join(flags, m_m, m_s)
    scaled = dy * vec[7:8, :]
    sums_o[0:1, :] = col_sum(scaled)
    sums_o[1:2, :] = col_sum(dy * (m + vec[6:7, :]))
    dm = scaled.astype(LOW)
    dm_o[...] = dm
    width = fc1.shape[1]
    chunk = min(width, 256)
    total = None
    for c in range(0, width, chunk):
        cut = slice(c, c + chunk)
        du = (dot_nt(dm, fc2[cut, :]) * dg[:, cut].astype(F32)).astype(LOW)
        du_o[:, cut] = du
        sums_o[2:3, cut] = col_sum(du.astype(F32))
        term = dot_nt(du, fc1[:, cut])
        total = term if total is None else total + term
    split_out(flags, total, mine_o, send_o)


def attn_bwd_kernel(
    seq, flags, x, a_m, a_s, dy, d_m, d_s, qkv, vec, wqkv, wout, dh_o, da_o, dqkv_o, mine_o, send_o, sums_o, pair_o
):
    a = join(flags, a_m, a_s) + vec[2:3, :]
    h1 = x[...].astype(F32) + vec[3:4, :] * a
    unit, inverse = unit_rows_of(h1)
    dn2 = join(flags, d_m, d_s)
    sums_o[0:1, :] = col_sum(dn2 * unit)
    sums_o[1:2, :] = col_sum(dn2)
    dh1 = dy[...].astype(F32) + norm_back(dn2, unit, inverse, vec[4:5, :])
    dh_o[...] = dh1
    scaled = dh1 * vec[3:4, :]
    sums_o[2:3, :] = col_sum(scaled)
    sums_o[3:4, :] = col_sum(dh1 * a)
    da = scaled.astype(LOW)
    da_o[...] = da
    do = dot_nt(da, wout[...]).astype(LOW)
    share = wqkv.shape[2]
    dqs, dks, dvs = [], [], []
    for h in range(share // HD):
        cut = slice(h * HD, (h + 1) * HD)
        q = qkv[:, h * HD : (h + 1) * HD]
        k = qkv[:, share + h * HD : share + (h + 1) * HD]
        v = qkv[:, 2 * share + h * HD : 2 * share + (h + 1) * HD]
        p = probs_of(q, k, seq)
        dvs.append(dot_tn(p.astype(LOW), do[:, cut]))
        dp = dot_nt(do[:, cut], v)
        ds = (p * (dp - jnp.sum(p * dp, axis=-1, keepdims=True))).astype(LOW)
        dqs.append(dot_nn(ds, k) * HD ** (-0.5))
        dks.append(dot_tn(ds, q) * HD ** (-0.5))
    dq = jnp.concatenate(dqs, axis=1).astype(LOW)
    dk = jnp.concatenate(dks, axis=1).astype(LOW)
    dv = jnp.concatenate(dvs, axis=1).astype(LOW)
    dqkv_o[:, 0:share] = dq
    dqkv_o[:, share : 2 * share] = dk
    dqkv_o[:, 2 * share :] = dv
    pair_o[0:1, :] = col_sum(dq.astype(F32))
    pair_o[1:2, :] = col_sum(dv.astype(F32))
    split_out(flags, dot_nt(dq, wqkv[0]) + dot_nt(dk, wqkv[1]) + dot_nt(dv, wqkv[2]), mine_o, send_o)


def in_bwd_kernel(flags, x, dh, d_m, d_s, vec, dx_o, low_o, sums_o):
    unit, inverse = unit_rows_of(x[...].astype(F32))
    dn1 = join(flags, d_m, d_s)
    sums_o[0:1, :] = col_sum(dn1 * unit)
    sums_o[1:2, :] = col_sum(dn1)
    dx = dh[...] + norm_back(dn1, unit, inverse, vec[0:1, :])
    dx_o[...] = dx[: dx_o.shape[0]]
    low_o[...] = own_half(flags, dx)


def weight_kernel(count, *refs):
    lefts, rights, out = refs[:count], refs[count : 2 * count], refs[2 * count + 1]
    total = dot_tn(lefts[0][...], rights[0][...])
    for n in range(1, count):
        total = total + dot_tn(lefts[n][...], rights[n][...])
    out[0] = total.astype(out.dtype)


def whole(shape, block=None, pick=None):
    block = shape if block is None else block
    at = (0,) * len(shape) if pick is None else pick
    return pl.BlockSpec(block, lambda i: at)


def skip_last(kernel, at, *refs):
    kernel(*refs[:at], *refs[at + 1 :])


def call(kernel, args, outs, after, picks=None, flops=0):
    picks = picks or {}
    specs = [pl.BlockSpec(memory_space=pltpu.SMEM)]
    for n, arg in enumerate(args[1:], 1):
        if n in picks:
            specs.append(whole(arg.shape, (1,) + arg.shape[1:], (picks[n], 0, 0)))
        else:
            specs.append(whole(arg.shape))
    specs.append(pl.BlockSpec(memory_space=pl.ANY))
    moved = sum(a.size * a.dtype.itemsize for a in args[1:])
    return pl.pallas_call(
        partial(skip_last, kernel, len(args)),
        grid=(1,),
        in_specs=specs,
        out_specs=[whole(s.shape) for s in outs],
        out_shape=outs,
        compiler_params=pltpu.CompilerParams(vmem_limit_bytes=VMEM_BYTES),
        cost_estimate=pl.CostEstimate(flops=flops, bytes_accessed=moved, transcendentals=0),
    )(*args, after)


def weight_grad(lefts, rights, blocks, after):
    count = len(lefts)
    rows, depth = lefts[0].shape
    width = rights[0].shape[1]
    block = width // blocks
    return pl.pallas_call(
        partial(weight_kernel, count),
        grid=(blocks,),
        in_specs=[pl.BlockSpec((rows, depth), lambda i: (0, 0))] * count
        + [pl.BlockSpec((rows, block), lambda i: (0, i))] * count
        + [pl.BlockSpec(memory_space=pl.ANY)],
        out_specs=pl.BlockSpec((1, depth, block), lambda i: (i, 0, 0)),
        out_shape=jax.ShapeDtypeStruct((blocks, depth, block), LOW),
        compiler_params=pltpu.CompilerParams(vmem_limit_bytes=VMEM_BYTES),
        cost_estimate=pl.CostEstimate(
            flops=2 * count * rows * depth * width,
            bytes_accessed=2 * count * rows * (depth + width) + 2 * depth * width,
            transcendentals=0,
        ),
    )(*lefts, *rights, after)


def pass_kernel(value, after, out):
    pass


def held_until(value, after):
    return pl.pallas_call(
        pass_kernel,
        in_specs=[pl.BlockSpec(memory_space=pl.ANY)] * 2,
        out_specs=pl.BlockSpec(memory_space=pl.ANY),
        out_shape=jax.ShapeDtypeStruct(value.shape, value.dtype),
        input_output_aliases={0: 0},
    )(value, after)


def swap(value, bit):
    route = [(i, i ^ bit) for i in range(lax.axis_size("tensor"))]
    return lax.ppermute(value, "tensor", route)


def tensor_sum(mine, send):
    size = lax.axis_size("tensor")
    got = swap(send, 1)
    first = held = (mine.astype(F32) + got.astype(F32)).astype(LOW)
    bit = 2
    while bit < size:
        got = swap(held, bit)
        held = (held.astype(F32) + got.astype(F32)).astype(LOW)
        bit *= 2
    return held, swap(held, 1), first


def passed_along(block, distance):
    devices = range(lax.axis_size("section"))
    route = [(i - distance, i) for i in devices if i - distance in devices]
    arrived = lax.ppermute(block, "section", route)
    return arrived, swap(arrived, 1)


def body(tokens, cotangent, vectors, w_qkv, qv_bias, w_out, w_fc1, fc1_bias, w_fc2):
    micro_count, images, seq, width = tokens.shape
    units = micro_count * images
    rows = -(-seq // 16) * 16
    wqkv, wout, fc1, fc2 = w_qkv[0], w_out[0], w_fc1[0], w_fc2[0]
    share, hidden = wqkv.shape[2], fc1.shape[1]
    vec = vectors[0].astype(F32)
    qvb = qv_bias[0].astype(F32)
    fc1b = fc1_bias.astype(F32)
    first = lax.axis_index("section") == 0
    flags = jnp.stack([first.astype(jnp.int32), (lax.axis_index("tensor") % 2).astype(jnp.int32)])
    pad = ((0, 0), (0, rows - seq), (0, 0))
    own = jnp.pad(tokens.reshape(units, seq, width), pad)
    cot = jnp.pad(cotangent.reshape(units, seq, width), pad)
    zeros = jnp.zeros((1, rows, width), LOW)
    nothing = (jnp.zeros((rows, width // 2), LOW),) * 2
    last = nothing[0]

    def low(*shape):
        return jax.ShapeDtypeStruct(shape, LOW)

    def wide(*shape):
        return jax.ShapeDtypeStruct(shape, F32)

    halves = [low(rows, width // 2)] * 2
    ticks = units + LAG
    unit_flops = 2 * rows * width
    arrivals, results, records = {}, [], []
    for start in range(0, ticks, LAG):
        group = range(start, min(start + LAG, ticks))
        kept = {}
        for t in group:
            x, n1, qkv, o, mine, send = call(
                partial(attn_fwd_kernel, seq),
                (flags, own if t < units else zeros, *arrivals.get(t, nothing), vec, wqkv, qvb, wout),
                [low(rows, width), low(rows, width), low(rows, 3 * share), low(rows, share)] + halves,
                last,
                {1: t} if t < units else None,
                unit_flops * share * 8,
            )
            a_m, a_s, last = tensor_sum(mine, send)
            kept[t] = (x, n1, qkv, o, a_m, a_s)
        for t in group:
            x, n1, qkv, o, a_m, a_s = kept[t]
            n2, g, dg, mine, send = call(
                mlp_fwd_kernel,
                (flags, x, a_m, a_s, vec, fc1, fc1b, fc2),
                [low(rows, width), low(rows, hidden), low(rows, hidden)] + halves,
                last,
                flops=unit_flops * hidden * 3,
            )
            m_m, m_s, last = tensor_sum(mine, send)
            kept[t] += (n2, g, dg, m_m, m_s)
        for t in group:
            x, a_m, a_s, m_m, m_s = [kept[t][n] for n in (0, 4, 5, 9, 10)]
            y, half = call(
                out_kernel,
                (flags, x, a_m, a_s, m_m, m_s, vec),
                [low(rows, width), low(rows, width // 2)],
                last,
            )
            results.append(y)
            if t + LAG < ticks:
                arrivals[t + LAG] = passed_along(half, 1)
            records.append(kept[t])

    returns, grads, small = {}, [], []
    pieces = [[] for _ in range(4)]
    for start in range(0, ticks, LAG):
        group = range(start, min(start + LAG, ticks))
        kept = {}
        for t in group:
            g, dg, m_m, m_s = records[ticks - 1 - t][7:]
            dy, dm, du, mine, send, sums_mlp = call(
                mlp_bwd_kernel,
                (flags, cot if t < units else zeros, *returns.get(t, nothing), m_m, m_s, dg, vec, fc1, fc2),
                [low(rows, width), low(rows, width), low(rows, hidden)] + halves + [wide(3, width)],
                last,
                {1: units - 1 - t} if t < units else None,
                unit_flops * hidden * 2,
            )
            d_m, d_s, last = tensor_sum(mine, send)
            kept[t] = (dy, d_m, d_s, sums_mlp)
            pieces[0].append((g, dm))
            pieces[1].append((records[ticks - 1 - t][6], du))
        for t in group:
            x, n1, qkv, o, a_m, a_s = records[ticks - 1 - t][:6]
            dy, d_m, d_s, sums_mlp = kept[t]
            dh, da, dqkv, mine, send, sums_attn, pair = call(
                partial(attn_bwd_kernel, seq),
                (flags, x, a_m, a_s, dy, d_m, d_s, qkv, vec, wqkv, wout),
                [wide(rows, width), low(rows, width), low(rows, 3 * share)]
                + halves
                + [wide(4, width), wide(2, share)],
                last,
                flops=unit_flops * share * 10,
            )
            d_m, d_s, last = tensor_sum(mine, send)
            kept[t] = (dh, d_m, d_s, sums_mlp, sums_attn, pair)
            pieces[2].append((o, da))
            pieces[3].append((n1, dqkv))
        for t in group:
            dh, d_m, d_s, sums_mlp, sums_attn, pair = kept[t]
            dx, half, sums_in = call(
                in_bwd_kernel,
                (flags, records[ticks - 1 - t][0], dh, d_m, d_s, vec),
                [wide(seq, width), low(rows, width // 2), wide(2, width)],
                last,
            )
            grads.append(dx)
            if t + LAG < ticks:
                returns[t + LAG] = passed_along(half, -1)
            small.append((sums_mlp, sums_attn, sums_in, pair))

    def grad_of(piece, blocks, after):
        return weight_grad([p[0] for p in piece], [p[1] for p in piece], blocks, after)

    grad_fc2 = grad_of(pieces[0], 2, last)
    grad_fc1 = grad_of(pieces[1], 2, last)
    grad_fc2, grad_fc1 = lax.psum((grad_fc2, grad_fc1), "dp")
    grad_out = grad_of(pieces[2], 2, last)
    grad_qkv = grad_of(pieces[3], 3, last)
    sums_mlp, sums_attn, sums_in, pair = [sum(s[1:], s[0]) for s in zip(*small)]
    rest = pair.size
    tail_rows = 9 + -(-rest // width)
    tail = jnp.concatenate(
        [
            sums_in,
            sums_attn[2:4],
            sums_attn[0:2],
            sums_mlp,
            jnp.pad(pair.reshape(-1), (0, (tail_rows - 9) * width - rest)).reshape(-1, width),
        ],
        axis=0,
    )
    tail_rows = -(-tail_rows // 16) * 16
    tail = jnp.pad(tail, ((0, tail_rows - tail.shape[0]), (0, 0))).astype(LOW)
    grad_out = jnp.concatenate([grad_out, tail.reshape(tail_rows, 2, -1).swapaxes(0, 1)], axis=1)
    grad_out, grad_qkv = lax.psum(
        tuple(held_until(held_until(g, grad_fc1), grad_fc2) for g in (grad_out, grad_qkv)), "dp"
    )
    tail = grad_out[:, share:].swapaxes(0, 1).reshape(tail_rows, width).astype(F32)
    grad_out = grad_out[:, :share]
    grad_vec, grad_fc1b = tail[0:8], tail[8:9]
    grad_pair = tail[9:].reshape(-1)[:rest].reshape(pair.shape)
    grad_fc2, grad_fc1, grad_qkv, grad_out = [
        g.astype(F32) for g in (grad_fc2, grad_fc1, grad_qkv, grad_out)
    ]

    def columns(blocked):
        return jnp.concatenate([blocked[n] for n in range(blocked.shape[0])], axis=1)

    shape_out = (1, micro_count, images, seq, width)
    outputs = jnp.stack(
        [jnp.where(first, results[m][:seq], results[m + LAG][:seq]) for m in range(units)]
    ).reshape(shape_out)
    input_grads = jnp.stack(
        [jnp.where(first, grads[ticks - 1 - m], grads[units - 1 - m]) for m in range(units)]
    ).reshape(shape_out)
    return (
        outputs,
        input_grads,
        grad_vec[None],
        grad_qkv[None],
        grad_pair[None],
        columns(grad_out)[None],
        columns(grad_fc1)[None],
        grad_fc1b,
        columns(grad_fc2)[None],
    )


def solution(mesh):
    return jax.shard_map(
        body,
        mesh=mesh,
        in_specs=(
            P(None, "dp", None, None),
            P(None, "dp", None, None),
            P("section", None, None),
            P("section", None, None, "tensor"),
            P("section", None, "tensor"),
            P("section", "tensor", None),
            P("section", None, "tensor"),
            P("section", "tensor"),
            P("section", "tensor", None),
        ),
        out_specs=(
            P("section", None, "dp", None, None),
            P("section", None, "dp", None, None),
            P("section", None, None),
            P("section", None, None, "tensor"),
            P("section", None, "tensor"),
            P("section", "tensor", None),
            P("section", None, "tensor"),
            P("section", "tensor"),
            P("section", "tensor", None),
        ),
        check_vma=False,
    )
```
